32 devices in a mesh: parts: 1, store: 8 (over z, y), tensor: 4 (over x, core), sub: 1.
Axes of the slice: x: 2, y: 2, z: 4, core: 2. Of those that a mesh axis runs over, the one named last changes fastest.
Arguments:
- tokens: bfloat16 [8192, 8192], P(('parts', 'store', 'tensor')), may hold values from -6 to 6
- attention_norm_gain: float32 [8192], replicated, may hold values from 0.25 to 1.75
- key_weight: bfloat16 [8192, 1024], P(None, ('tensor', 'sub')), may hold values from -0.0625 to 0.0625
- value_weight: bfloat16 [8192, 1024], P(None, ('tensor', 'sub')), may hold values from -0.0625 to 0.0625
- adapter_down_weight: bfloat16 [24, 8192, 128], P(('parts', 'store'), ('tensor', 'sub')), may hold values from -0.0625 to 0.0625
- adapter_up_weight: bfloat16 [24, 2, 64, 1024], P(('parts', 'store'), None, None, ('tensor', 'sub')), may hold values from -0.75 to 0.75
- storage_slot_adapter: int32 [24], P('parts'), may hold values from 0 to 23, as said below
- request_adapter: int32 [48], P('parts'), may hold values from 0 to 23, as said below
- segment_blocks: int32 [8, 6], P(('parts', 'store')), may hold values from 1 to 2, 8 in all within a row
Outputs:
- keys: bfloat16 [8192, 1024], P(('parts', 'store'), ('tensor', 'sub'))
- values: bfloat16 [8192, 1024], P(('parts', 'store'), ('tensor', 'sub'))
The draws below stay inside these ranges and needn't reach their ends.
Inputs may be any that keep to these rules, and one draw needn't show every extreme that they name: `storage_slot_adapter`: a permutation: each adapter id stands in exactly one slot; slot q is stored on store index q // 3. `request_adapter`: requests g * 6 to (g + 1) * 6 - 1 belong to store group g; request j of store group g names an adapter stored on store index (g + n / 2 + j * (n / 2 - 1)) modulo n, with n the number of store indices. `segment_blocks`: row g holds the lengths of store group g's requests in order, in blocks of 128 rows; they add up to 8.
All inputs are finite; a program needn't handle non-finite values.
Results may differ from the reference program's by a relative error of at most 0.0051.
Values may be sent and summed in bfloat16 or wider, within the bound.
A program may use at most 128 MiB of HBM per device.

```python
import math
from functools import partial
import jax
import jax.numpy as jnp
import numpy as np
from jax import lax

MODEL_WIDTH = 8192
HD = 128
ADAPTER_RANK = 64
BLOCK = 128
ADP_ST = 3
KEY_COLUMNS = 1024
TOKENS = 8192
BLK_GRP = 8
SEG_GRP = 6
SEGMAX = 2
REQS = 48
ADAPTER_TOTAL = 24
N_STORE = 8


def slot_order(key):
    return jax.random.permutation(jax.random.fold_in(key, 17), ADAPTER_TOTAL).astype(jnp.int32)


def draw_storage_slot_adapter(key, part):
    order = slot_order(key)
    return order


def draw_request_adapter(key, part):
    order = slot_order(key)
    key = jax.random.fold_in(key, 5)
    group_total = ADAPTER_TOTAL // ADP_ST
    group_iota = jnp.arange(group_total, dtype=jnp.int32)
    seg_iota = jnp.arange(SEG_GRP, dtype=jnp.int32)
    offsets = (group_total // 2 + seg_iota * (group_total // 2 - 1)) % group_total
    owners = (group_iota[:, None] + offsets[None, :]) % group_total
    local_slot = jax.random.randint(jax.random.fold_in(key, 2), (group_total, SEG_GRP), 0, ADP_ST).astype(jnp.int32)
    return order[owners * ADP_ST + local_slot].reshape(REQS).astype(jnp.int32)


def steps_of(stream_key, extent, cuts, least, high):
    factor_of, own = 1.0, jax.random.fold_in(stream_key, 6)
    for dim, parts in cuts:
        heights = jnp.exp(jax.random.uniform(jax.random.fold_in(own, dim), (parts,), jnp.float32, least / len(cuts), high / len(cuts)))
        factor_of = factor_of * jnp.repeat(heights, extent[dim] // parts).reshape([-1 if axis == dim else 1 for axis in range(len(extent))])
    return factor_of


def length_profile(amount, total, bound, slope):
    loads = [(1 << 20) // math.isqrt(grade ** slope) + 1 for grade in range(2, amount + 1)]
    rest, counts = total - bound - (amount - 1), [1] * (amount - 1)
    while rest > 0:
        movable = [i for i in range(amount - 1) if counts[i] < bound]
        whole, remaining = sum([loads[i] for i in movable]), rest
        for i in movable:
            addition = min(bound - counts[i], max(1, remaining * loads[i] // whole), rest)
            counts[i] = counts[i] + addition
            rest = rest - addition
    return np.array([bound] + counts)


def uneven_parts(key, amount, total, reach, slope):
    if amount == 2:
        one = jax.random.randint(key, (), max(1, total - reach), min(reach, total - 1) + 1)
        return jnp.stack([one, total - one])
    sizes = jnp.asarray(length_profile(amount, total, reach, slope), jnp.int32)
    pairs = (amount - 1) // 2
    giver, receiver = sizes[1:1 + 2 * pairs:2], sizes[2:2 + 2 * pairs:2]
    margin = jnp.minimum(giver - 1, reach - receiver)
    moved = jax.random.randint(jax.random.fold_in(key, 1), (pairs,), 0, 1 << 20) % (margin + 1)
    sizes = sizes.at[1:1 + 2 * pairs:2].set(giver - moved).at[2:2 + 2 * pairs:2].set(receiver + moved)
    return sizes[jax.random.permutation(jax.random.fold_in(key, 2), amount)]


def gaussian(rng, shape, scale, bound, split=(), kind=jnp.bfloat16):
    drawn = scale * jax.random.normal(rng, shape, jnp.float32)
    if split:
        drawn = drawn * steps_of(rng, shape, split, -0.22, 0.18)
    return jnp.clip(drawn, -bound, bound).astype(kind)


def setup_inputs(seed: int = 0, part: int = 0) -> dict:
    key_of = jax.random.split(jax.random.key(seed), 10)
    part_splits = jax.random.split(jax.random.fold_in(key_of[9], part), 10)
    return {
        "tokens": gaussian(part_splits[0], (TOKENS, MODEL_WIDTH), 1.0, 6.0, ((0, 32),)),
        "attention_norm_gain": jnp.clip(1.0 + 0.15 * jax.random.normal(key_of[1], (MODEL_WIDTH,), jnp.float32), 0.25, 1.75),
        "key_weight": gaussian(key_of[2], (MODEL_WIDTH, KEY_COLUMNS), MODEL_WIDTH ** -0.5, 0.0625, ((1, 4),)),
        "value_weight": gaussian(key_of[3], (MODEL_WIDTH, KEY_COLUMNS), MODEL_WIDTH ** -0.5, 0.0625, ((1, 4),)),
        "adapter_down_weight": gaussian(part_splits[4], (ADAPTER_TOTAL, MODEL_WIDTH, 2 * ADAPTER_RANK), MODEL_WIDTH ** -0.5, 0.0625, ((0, 8), (1, 4))),
        "adapter_up_weight": gaussian(part_splits[5], (ADAPTER_TOTAL, 2, ADAPTER_RANK, KEY_COLUMNS), ADAPTER_RANK ** -0.5, 0.75, ((0, 8), (3, 4))),
        "storage_slot_adapter": draw_storage_slot_adapter(jax.random.fold_in(jax.random.fold_in(key_of[9], part), 71), part),
        "request_adapter": draw_request_adapter(jax.random.fold_in(jax.random.fold_in(key_of[9], part), 71), part),
        "segment_blocks": jax.vmap(lambda own: uneven_parts(own, SEG_GRP, BLK_GRP, SEGMAX, 0))(jax.random.split(part_splits[8], N_STORE)).reshape((N_STORE, SEG_GRP)).astype(jnp.int32),
    }


adapter_scale = 0.5
rope_base = 500000.0

def normalize(tokens, attention_norm_gain):
    wide = tokens.astype(jnp.float32)
    factor = lax.rsqrt(lax.optimization_barrier(jnp.mean(wide * wide, axis=1, keepdims=True)) + 1e-05)
    return (wide * factor * attention_norm_gain[None, :]).astype(jnp.bfloat16)

def apply_rotary(pre_rot, token_positions):
    row_count = pre_rot.shape[0]
    half_width = HD // 2
    frequency = rope_base ** (-2.0 * jnp.arange(half_width, dtype=jnp.float32) / HD)
    angles = token_positions.astype(jnp.float32)[:, None] * frequency[None, :]
    cosine_part = jnp.cos(angles)[:, None, :]
    sine_part = jnp.sin(angles)[:, None, :]
    heads = pre_rot.reshape(row_count, pre_rot.shape[1] // HD, HD)
    first_half = heads[:, :, :half_width]
    second_half = heads[:, :, half_width:]
    turned = jnp.concatenate([first_half * cosine_part - second_half * sine_part, second_half * cosine_part + first_half * sine_part], axis=2)
    return turned.reshape(row_count, pre_rot.shape[1])

def find_slots(adapter_ids, storage_slot_adapter):
    slot_iota = jnp.arange(storage_slot_adapter.shape[0], dtype=jnp.int32)
    hits = adapter_ids[..., None] == storage_slot_adapter
    return lax.optimization_barrier(jnp.sum(jnp.where(hits, slot_iota, 0), axis=-1)).astype(jnp.int32)

def block_layout(block_count, seg_row, group_req):
    seg_end = jnp.cumsum(seg_row).astype(jnp.int32)
    block_iota = jnp.arange(block_count, dtype=jnp.int32)
    which_seg = lax.optimization_barrier(jnp.sum((seg_end[None, :] <= block_iota[:, None]).astype(jnp.int32), axis=1)).astype(jnp.int32)
    seg_iota = jnp.arange(seg_row.shape[0], dtype=jnp.int32)
    picked = seg_iota[None, :] == which_seg[:, None]
    block_adapter = lax.optimization_barrier(jnp.sum(jnp.where(picked, group_req[None, :], 0), axis=1)).astype(jnp.int32)
    first_block = lax.optimization_barrier(jnp.sum(jnp.where(picked, (seg_end - seg_row)[None, :], 0), axis=1)).astype(jnp.int32)
    return (block_adapter, block_iota - first_block)

def reference(tokens, attention_norm_gain, key_weight, value_weight, adapter_down_weight, adapter_up_weight, storage_slot_adapter, request_adapter, segment_blocks):
    normed = normalize(tokens, attention_norm_gain)
    group_count = segment_blocks.shape[0]
    group_req = request_adapter.reshape(group_count, SEG_GRP)
    block_adapter, block_offset = jax.vmap(partial(block_layout, BLK_GRP))(segment_blocks, group_req)
    block_slot = find_slots(block_adapter.reshape(-1), storage_slot_adapter)
    row_iota = jnp.arange(BLOCK, dtype=jnp.int32)
    token_positions = (block_offset[:, :, None] * BLOCK + row_iota[None, None, :]).reshape(-1)
    plain_keys = jnp.dot(normed, key_weight, preferred_element_type=jnp.float32)
    plain_values = jnp.dot(normed, value_weight, preferred_element_type=jnp.float32)
    block_rows = normed.reshape(-1, BLOCK, MODEL_WIDTH)

    def one_block(item):
        row_block, storage_slot = item
        down_matrix = lax.dynamic_index_in_dim(adapter_down_weight, storage_slot.astype(jnp.int32), 0, keepdims=False)
        up_matrix = lax.dynamic_index_in_dim(adapter_up_weight, storage_slot.astype(jnp.int32), 0, keepdims=False)
        shrunk = jnp.dot(row_block, down_matrix, preferred_element_type=jnp.float32).astype(jnp.bfloat16)
        adapter_keys = jnp.dot(shrunk[:, :ADAPTER_RANK], up_matrix[0], preferred_element_type=jnp.float32)
        adapter_values = jnp.dot(shrunk[:, ADAPTER_RANK:], up_matrix[1], preferred_element_type=jnp.float32)
        return (adapter_keys, adapter_values)
    adapter_keys, adapter_values = lax.map(one_block, (block_rows, block_slot))
    unrotated_keys = plain_keys + adapter_scale * adapter_keys.reshape(-1, KEY_COLUMNS)
    keys = apply_rotary(unrotated_keys, token_positions).astype(jnp.bfloat16)
    values = (plain_values + adapter_scale * adapter_values.reshape(-1, KEY_COLUMNS)).astype(jnp.bfloat16)
    return (keys, values)
```

```python
import functools

import jax
import jax.numpy as jnp
import numpy as np
from jax import lax
from jax.experimental import pallas as pl
from jax.experimental.pallas import tpu as pltpu
from jax.sharding import PartitionSpec as P

HD = 128
ADAPTER_RANK = 64
BLOCK = 128


adapter_scale = 0.5
rope_base = 500000.0


def apply_rotary(pre_rot, token_positions):
    row_count = pre_rot.shape[0]
    half_width = HD // 2
    frequency = rope_base ** (-2.0 * jnp.arange(half_width, dtype=jnp.float32) / HD)
    angles = token_positions.astype(jnp.float32)[:, None] * frequency[None, :]
    cosine_part = jnp.cos(angles)[:, None, :]
    sine_part = jnp.sin(angles)[:, None, :]
    heads = pre_rot.reshape(row_count, pre_rot.shape[1] // HD, HD)
    first_half = heads[:, :, :half_width]
    second_half = heads[:, :, half_width:]
    turned = jnp.concatenate(
        [
            first_half * cosine_part - second_half * sine_part,
            second_half * cosine_part + first_half * sine_part,
        ],
        axis=2,
    )
    return turned.reshape(row_count, pre_rot.shape[1])


def find_slots(adapter_ids, storage_slot_adapter):
    slot_iota = jnp.arange(storage_slot_adapter.shape[0], dtype=jnp.int32)
    hits = adapter_ids[..., None] == storage_slot_adapter
    return jnp.sum(jnp.where(hits, slot_iota, 0), axis=-1)


def block_layout(block_count, seg_row, group_req):
    seg_end = jnp.cumsum(seg_row)
    block_iota = jnp.arange(block_count, dtype=jnp.int32)
    which_seg = jnp.sum((seg_end[None, :] <= block_iota[:, None]).astype(jnp.int32), axis=1)
    seg_iota = jnp.arange(seg_row.shape[0], dtype=jnp.int32)
    picked = seg_iota[None, :] == which_seg[:, None]
    block_adapter = jnp.sum(jnp.where(picked, group_req[None, :], 0), axis=1)
    first_block = jnp.sum(jnp.where(picked, (seg_end - seg_row)[None, :], 0), axis=1)
    return (block_adapter, block_iota - first_block)


def per_device(
    tokens,
    attention_norm_gain,
    key_weight,
    value_weight,
    adapter_down_weight,
    adapter_up_weight,
    storage_slot_adapter,
    request_adapter,
    segment_blocks,
):
    wide = tokens.astype(jnp.float32)
    factor = lax.rsqrt(jnp.mean(wide * wide, axis=1, keepdims=True) + 1e-05)
    normed = (wide * factor * attention_norm_gain[None, :]).astype(jnp.bfloat16)
    shared_width = adapter_down_weight.shape[1]
    column_width = key_weight.shape[1]
    feature_start = lax.axis_index(("tensor", "sub")) * shared_width
    piece = lax.all_gather(normed, "tensor", axis=0, tiled=True)
    keys_part = jnp.dot(piece, key_weight, preferred_element_type=jnp.float32)
    values_part = jnp.dot(piece, value_weight, preferred_element_type=jnp.float32)
    feature_cols = lax.dynamic_slice_in_dim(piece, feature_start, shared_width, 1).astype(
        jnp.float32
    )
    gathered = jnp.concatenate([keys_part, values_part, feature_cols], axis=1)
    plain_keys = gathered[:, :column_width]
    plain_values = gathered[:, column_width : 2 * column_width]
    feature_rows = gathered[:, 2 * column_width :].astype(jnp.bfloat16)
    block_count = gathered.shape[0] // BLOCK
    seg_count = segment_blocks.shape[1]
    group = lax.axis_index("store")
    group_req = lax.dynamic_slice_in_dim(request_adapter, group * seg_count, seg_count)
    block_adapter, block_offset = block_layout(block_count, segment_blocks[0], group_req)
    block_slot = find_slots(block_adapter, storage_slot_adapter)
    down_table, up_table = (
        lax.all_gather(adapter_down_weight, "store", axis=0, tiled=True),
        lax.all_gather(adapter_up_weight, "store", axis=0, tiled=True),
    )
    block_down = down_table[block_slot]
    block_up = up_table[block_slot]
    partial_sum = jnp.einsum(
        "bnd,bdk->bnk",
        feature_rows.reshape(block_count, BLOCK, shared_width),
        block_down,
        preferred_element_type=jnp.float32,
    ).reshape(block_count * BLOCK, 2 * ADAPTER_RANK)
    shrunk = lax.psum(partial_sum, ("tensor", "sub")).astype(jnp.bfloat16)
    delta = jnp.einsum(
        "bnsr,bsrc->sbnc",
        shrunk.reshape(block_count, BLOCK, 2, ADAPTER_RANK),
        block_up,
        preferred_element_type=jnp.float32,
    )
    adapter_keys = delta[0].reshape(-1, column_width)
    adapter_values = delta[1].reshape(-1, column_width)
    row_iota = jnp.arange(BLOCK, dtype=jnp.int32)
    token_positions = (block_offset[:, None] * BLOCK + row_iota[None, :]).reshape(-1)
    keys = apply_rotary(plain_keys + adapter_scale * adapter_keys, token_positions).astype(
        jnp.bfloat16
    )
    values = (plain_values + adapter_scale * adapter_values).astype(jnp.bfloat16)
    return (keys, values)


CHUNK = 32


def fused_kernel(
    n_store,
    tok_hbm, gain, kw_hbm, vw_hbm, down_hbm, up_hbm, slots, req, seg, cos_ref, sin_ref,
    keys_out, vals_out,
    tok, rows, kw, vw, down, up, sdown, sup, rdown, rup, acck, accv, part, rs1, mid, rs2, sh,
    tok_sem, w_sem, xs_sem, xr_sem, ss_sem, sr_sem, fs_sem, fr_sem,
    ds_sem, dr_sem, us_sem, ur_sem, es_sem, er_sem,
):
    n_chunk = rows.shape[1]
    shard = n_chunk * CHUNK
    seg_count = rdown.shape[0]
    stored = down.shape[0]
    depth = down.shape[1]
    n_block = part.shape[0]
    half = n_block // 2
    store = lax.axis_index("store")
    t = lax.axis_index("tensor")
    x, c = t // 2, t % 2
    ox, oc = 1 - x, 1 - c
    peer = {"tensor": ox * 2 + c}
    sibling = {"tensor": x * 2 + oc}
    offsets = [(n_store // 2 + j * (n_store // 2 - 1)) % n_store for j in range(seg_count)]
    remote = [j for j in range(seg_count) if offsets[j] != 0]

    def dst_of(j):
        return lax.rem(store + (n_store - offsets[j]), n_store)

    def src_of(j):
        return lax.rem(store + offsets[j], n_store)

    def tok_copy(k):
        r = pl.ds(pl.multiple_of(k * CHUNK, CHUNK), CHUNK)
        return pltpu.make_async_copy(tok_hbm.at[r], tok.at[r], tok_sem.at[k])

    loads = [
        pltpu.make_async_copy(down_hbm, down, w_sem.at[0]),
        pltpu.make_async_copy(up_hbm, up, w_sem.at[1]),
        pltpu.make_async_copy(kw_hbm, kw, w_sem.at[2]),
        pltpu.make_async_copy(vw_hbm, vw, w_sem.at[3]),
    ]
    tok_copy(0).start()
    loads[0].start()
    loads[1].start()
    for k in range(1, n_chunk):
        tok_copy(k).start()
    loads[2].start()
    loads[3].start()

    barrier = pltpu.get_barrier_semaphore()
    greet = [peer, sibling]
    for j in remote:
        greet += [{"store": dst_of(j)}, {"store": src_of(j)}]
    for who in greet:
        pl.semaphore_signal(barrier, inc=1, device_id=who, device_id_type=pl.DeviceIdType.MESH)

    def remote_copy(src, dst, ssem, rsem, who):
        return pltpu.make_async_remote_copy(
            src_ref=src, dst_ref=dst, send_sem=ssem, recv_sem=rsem,
            device_id=who, device_id_type=pl.DeviceIdType.MESH,
        )

    def x_copy(k):
        return remote_copy(rows.at[x, k, c], rows.at[x, k, c], xs_sem.at[k], xr_sem.at[k], peer)

    def s_copy(k):
        return remote_copy(rows.at[x, k, c], rows.at[x, k, c], ss_sem.at[k], sr_sem.at[k], sibling)

    def f_copy(k):
        return remote_copy(rows.at[ox, k, c], rows.at[ox, k, c], fs_sem.at[k], fr_sem.at[k], sibling)

    def d_copy(j):
        return remote_copy(sdown.at[j], rdown.at[j], ds_sem.at[j], dr_sem.at[j], {"store": dst_of(j)})

    def u_copy(j):
        return remote_copy(sup.at[j], rup.at[j], us_sem.at[j], ur_sem.at[j], {"store": dst_of(j)})

    def normalize(k):
        tok_copy(k).wait()

        def group(i, carry):
            r = pl.ds(pl.multiple_of(k * CHUNK + i * 16, 16), 16)
            wide = tok[r, :].astype(jnp.float32)
            factor = lax.rsqrt(jnp.mean(wide * wide, axis=1, keepdims=True) + 1e-05)
            rows[x, k, c, pl.ds(pl.multiple_of(i * 16, 16), 16), :] = (
                wide * factor * gain[...]
            ).astype(jnp.bfloat16)
            return carry

        lax.fori_loop(0, CHUNK // 16, group, 0)

    normalize(0)
    pl.semaphore_wait(barrier, len(greet))
    x_copy(0).start()
    s_copy(0).start()

    loads[0].wait()
    loads[1].wait()
    for j in range(seg_count):
        wanted = req[dst_of(j) * seg_count + j]
        local = jnp.int32(0)
        for i in range(1, stored):
            local = jnp.where(slots[store * stored + i] == wanted, jnp.int32(i), local)
        if j in remote:
            sdown[j] = down[local]
            sup[j] = up[local]
            d_copy(j).start()
            u_copy(j).start()
        else:
            rdown[j] = down[local]
            rup[j] = up[local]

    normalize(1)
    x_copy(1).start()
    s_copy(1).start()

    def prepare(k, carry):
        normalize(k)
        s_copy(k).start()
        return carry

    lax.fori_loop(2, n_chunk, prepare, 0)

    loads[2].wait()
    loads[3].wait()

    def project(xi, k, ci, count):
        at = pl.ds(pl.multiple_of((xi * 2 + ci) * shard + k * CHUNK, CHUNK), count * CHUNK)
        lhs = rows[xi, pl.ds(k, count), ci].reshape(count * CHUNK, kw.shape[0])
        acck[at, :] = jnp.dot(lhs, kw[...], preferred_element_type=jnp.float32)
        accv[at, :] = jnp.dot(lhs, vw[...], preferred_element_type=jnp.float32)

    group = 4

    def local_rows(i, carry):
        project(x, i * group, c, group)
        return carry

    lax.fori_loop(0, n_chunk // group, local_rows, 0)

    def sibling_rows(i, carry):
        def arrived(k, inner):
            s_copy(i * group + k).wait()
            return inner

        lax.fori_loop(0, group, arrived, 0)
        project(x, i * group, oc, group)
        return carry

    lax.fori_loop(0, n_chunk // group, sibling_rows, 0)

    def far_rows(k, carry):
        x_copy(k).wait()
        f_copy(k).start()

        @pl.when(k + 2 < n_chunk)
        def _():
            x_copy(k + 2).start()

        f_copy(k).wait()
        lhs = rows[ox, k].reshape(2 * CHUNK, kw.shape[0])
        pk = jnp.dot(lhs, kw[...], preferred_element_type=jnp.float32)
        pv = jnp.dot(lhs, vw[...], preferred_element_type=jnp.float32)
        for ci in range(2):
            at = pl.ds(pl.multiple_of((ox * 2 + ci) * shard + k * CHUNK, CHUNK), CHUNK)
            acck[at, :] = pk[ci * CHUNK : (ci + 1) * CHUNK]
            accv[at, :] = pv[ci * CHUNK : (ci + 1) * CHUNK]
        return carry

    lax.fori_loop(0, n_chunk, far_rows, 0)

    for j in remote:
        d_copy(j).wait()
        u_copy(j).wait()

    def layout(b):
        end, which, first = jnp.int32(0), jnp.int32(0), jnp.int32(0)
        for j in range(seg_count):
            end = end + seg[0, j]
            past = end <= b
            which = which + jnp.where(past, jnp.int32(1), jnp.int32(0))
            first = jnp.where(past, end, first)
        return jnp.minimum(which, seg_count - 1), jnp.minimum(b - first, cos_ref.shape[0] - 1)

    per_block = BLOCK // CHUNK
    per_shard = shard // BLOCK

    def shrink(b, carry):
        which, _ = layout(b)
        ti = b // per_shard
        k0 = (b % per_shard) * per_block
        feats = pl.ds(pl.multiple_of(t * depth, depth), depth)
        lhs = rows[ti // 2, pl.ds(k0, per_block), ti % 2, :, feats].reshape(BLOCK, depth)
        part[b] = jnp.dot(lhs, rdown[which], preferred_element_type=jnp.float32)
        return carry

    lax.fori_loop(0, n_block, shrink, 0)

    mine = pl.ds(c * half, half)
    others = pl.ds(oc * half, half)
    e0 = remote_copy(part.at[others], rs1, es_sem.at[0], er_sem.at[0], sibling)
    e0.start()
    e0.wait()
    mid[...] = part[mine] + rs1[...]
    e1 = remote_copy(mid, rs2, es_sem.at[1], er_sem.at[1], peer)
    e1.start()
    e1.wait()
    sh[mine] = (mid[...] + rs2[...]).astype(jnp.bfloat16)
    e2 = remote_copy(sh.at[mine], sh.at[mine], es_sem.at[2], er_sem.at[2], sibling)
    e2.start()
    e2.wait()

    def finish(b, carry):
        which, place = layout(b)
        at = pl.ds(pl.multiple_of(b * BLOCK, BLOCK), BLOCK)
        low = sh[b]
        dk = jnp.dot(low[:, :ADAPTER_RANK], rup[which, 0], preferred_element_type=jnp.float32)
        dv = jnp.dot(low[:, ADAPTER_RANK:], rup[which, 1], preferred_element_type=jnp.float32)
        vals_out[at, :] = (accv[at, :] + adapter_scale * dv).astype(jnp.bfloat16)
        p = acck[at, :] + adapter_scale * dk
        cos, sin = cos_ref[place], sin_ref[place]
        for h in range(p.shape[1] // HD):
            head = p[:, h * HD : (h + 1) * HD]
            turned = head * cos + pltpu.roll(head, HD // 2, 1) * sin
            keys_out[at, h * HD : (h + 1) * HD] = turned.astype(jnp.bfloat16)
        return carry

    lax.fori_loop(0, n_block, finish, 0)


def rotary_tables(blocks):
    frequency = np.float32(rope_base) ** (
        np.float32(-2.0) * np.arange(HD // 2, dtype=np.float32) / np.float32(HD)
    )
    angles = np.arange(blocks * BLOCK, dtype=np.float32)[:, None] * frequency[None, :]
    wide = angles.astype(np.float64)
    cos = np.concatenate([np.cos(wide), np.cos(wide)], axis=1).astype(np.float32)
    sin = np.concatenate([-np.sin(wide), np.sin(wide)], axis=1).astype(np.float32)
    return cos.reshape(blocks, BLOCK, HD), sin.reshape(blocks, BLOCK, HD)


def fused(
    n_store,
    tokens,
    attention_norm_gain,
    key_weight,
    value_weight,
    adapter_down_weight,
    adapter_up_weight,
    storage_slot_adapter,
    request_adapter,
    segment_blocks,
):
    shard, width = tokens.shape
    cols = key_weight.shape[1]
    total = 4 * shard
    n_chunk = shard // CHUNK
    n_block = total // BLOCK
    seg_count = segment_blocks.shape[1]
    stored, depth, ranks = adapter_down_weight.shape
    up_shape = adapter_up_weight.shape[1:]
    cos, sin = rotary_tables(n_block - seg_count + 1)
    bf16, f32 = jnp.bfloat16, jnp.float32
    any_spec = pl.BlockSpec(memory_space=pl.ANY)
    vmem = pl.BlockSpec(memory_space=pltpu.VMEM)
    smem = pl.BlockSpec(memory_space=pltpu.SMEM)
    dma = pltpu.SemaphoreType.DMA
    half = n_block // 2
    return pl.pallas_call(
        functools.partial(fused_kernel, n_store),
        out_shape=[jax.ShapeDtypeStruct((total, cols), bf16)] * 2,
        in_specs=[any_spec, vmem, any_spec, any_spec, any_spec, any_spec, smem, smem, smem, vmem, vmem],
        out_specs=[vmem, vmem],
        scratch_shapes=[
            pltpu.VMEM((shard, width), bf16),
            pltpu.VMEM((2, n_chunk, 2, CHUNK, width), bf16),
            pltpu.VMEM((width, cols), bf16),
            pltpu.VMEM((width, cols), bf16),
            pltpu.VMEM((stored, depth, ranks), bf16),
            pltpu.VMEM((stored,) + up_shape, bf16),
            pltpu.VMEM((seg_count, depth, ranks), bf16),
            pltpu.VMEM((seg_count,) + up_shape, bf16),
            pltpu.VMEM((seg_count, depth, ranks), bf16),
            pltpu.VMEM((seg_count,) + up_shape, bf16),
            pltpu.VMEM((total, cols), f32),
            pltpu.VMEM((total, cols), f32),
            pltpu.VMEM((n_block, BLOCK, ranks), f32),
            pltpu.VMEM((half, BLOCK, ranks), f32),
            pltpu.VMEM((half, BLOCK, ranks), f32),
            pltpu.VMEM((half, BLOCK, ranks), f32),
            pltpu.VMEM((n_block, BLOCK, ranks), bf16),
            dma((n_chunk,)), dma((4,)), dma((n_chunk,)), dma((n_chunk,)), dma((n_chunk,)),
            dma((n_chunk,)), dma((n_chunk,)), dma((n_chunk,)),
            dma((seg_count,)), dma((seg_count,)), dma((seg_count,)), dma((seg_count,)),
            dma((3,)), dma((3,)),
        ],
        compiler_params=pltpu.CompilerParams(
            collective_id=0, has_side_effects=True, vmem_limit_bytes=56 * 1024 * 1024
        ),
        cost_estimate=pl.CostEstimate(
            flops=2 * total * (2 * width * cols + depth * ranks),
            bytes_accessed=2 * (shard * width + 2 * width * cols + 2 * total * cols),
            transcendentals=0,
        ),
    )(
        tokens,
        attention_norm_gain.reshape(1, width),
        key_weight,
        value_weight,
        adapter_down_weight,
        adapter_up_weight,
        storage_slot_adapter,
        request_adapter,
        segment_blocks,
        jnp.asarray(cos),
        jnp.asarray(sin),
    )


def solution(mesh):
    in_specs = (
        P(("parts", "store", "tensor"), None),
        P(),
        P(None, ("tensor", "sub")),
        P(None, ("tensor", "sub")),
        P(("parts", "store"), ("tensor", "sub"), None),
        P(("parts", "store"), None, None, ("tensor", "sub")),
        P("parts"),
        P("parts"),
        P(("parts", "store"), None),
    )
    out_specs = (P(("parts", "store"), ("tensor", "sub")), P(("parts", "store"), ("tensor", "sub")))
    body = per_device
    if mesh.shape["sub"] == 1 and mesh.shape["tensor"] == 4:
        body = functools.partial(fused, mesh.shape["store"])
    return jax.shard_map(
        body, mesh=mesh, in_specs=in_specs, out_specs=out_specs, check_vma=False
    )
```

```python
import functools

import jax
import jax.numpy as jnp
import numpy as np
from jax import lax
from jax.experimental import pallas as pl
from jax.experimental.pallas import tpu as pltpu
from jax.sharding import PartitionSpec as P

HD = 128
ADAPTER_RANK = 64
BLOCK = 128


adapter_scale = 0.5
rope_base = 500000.0


def apply_rotary(pre_rot, token_positions):
    row_count = pre_rot.shape[0]
    half_width = HD // 2
    frequency = rope_base ** (-2.0 * jnp.arange(half_width, dtype=jnp.float32) / HD)
    angles = token_positions.astype(jnp.float32)[:, None] * frequency[None, :]
    cosine_part = jnp.cos(angles)[:, None, :]
    sine_part = jnp.sin(angles)[:, None, :]
    heads = pre_rot.reshape(row_count, pre_rot.shape[1] // HD, HD)
    first_half = heads[:, :, :half_width]
    second_half = heads[:, :, half_width:]
    turned = jnp.concatenate(
        [
            first_half * cosine_part - second_half * sine_part,
            second_half * cosine_part + first_half * sine_part,
        ],
        axis=2,
    )
    return turned.reshape(row_count, pre_rot.shape[1])


def find_slots(adapter_ids, storage_slot_adapter):
    slot_iota = jnp.arange(storage_slot_adapter.shape[0], dtype=jnp.int32)
    hits = adapter_ids[..., None] == storage_slot_adapter
    return jnp.sum(jnp.where(hits, slot_iota, 0), axis=-1)


def block_layout(block_count, seg_row, group_req):
    seg_end = jnp.cumsum(seg_row)
    block_iota = jnp.arange(block_count, dtype=jnp.int32)
    which_seg = jnp.sum((seg_end[None, :] <= block_iota[:, None]).astype(jnp.int32), axis=1)
    seg_iota = jnp.arange(seg_row.shape[0], dtype=jnp.int32)
    picked = seg_iota[None, :] == which_seg[:, None]
    block_adapter = jnp.sum(jnp.where(picked, group_req[None, :], 0), axis=1)
    first_block = jnp.sum(jnp.where(picked, (seg_end - seg_row)[None, :], 0), axis=1)
    return (block_adapter, block_iota - first_block)


def per_device(
    tokens,
    attention_norm_gain,
    key_weight,
    value_weight,
    adapter_down_weight,
    adapter_up_weight,
    storage_slot_adapter,
    request_adapter,
    segment_blocks,
):
    wide = tokens.astype(jnp.float32)
    factor = lax.rsqrt(jnp.mean(wide * wide, axis=1, keepdims=True) + 1e-05)
    normed = (wide * factor * attention_norm_gain[None, :]).astype(jnp.bfloat16)
    shared_width = adapter_down_weight.shape[1]
    column_width = key_weight.shape[1]
    feature_start = lax.axis_index(("tensor", "sub")) * shared_width
    piece = lax.all_gather(normed, "tensor", axis=0, tiled=True)
    keys_part = jnp.dot(piece, key_weight, preferred_element_type=jnp.float32)
    values_part = jnp.dot(piece, value_weight, preferred_element_type=jnp.float32)
    feature_cols = lax.dynamic_slice_in_dim(piece, feature_start, shared_width, 1).astype(
        jnp.float32
    )
    gathered = jnp.concatenate([keys_part, values_part, feature_cols], axis=1)
    plain_keys = gathered[:, :column_width]
    plain_values = gathered[:, column_width : 2 * column_width]
    feature_rows = gathered[:, 2 * column_width :].astype(jnp.bfloat16)
    block_count = gathered.shape[0] // BLOCK
    seg_count = segment_blocks.shape[1]
    group = lax.axis_index("store")
    group_req = lax.dynamic_slice_in_dim(request_adapter, group * seg_count, seg_count)
    block_adapter, block_offset = block_layout(block_count, segment_blocks[0], group_req)
    block_slot = find_slots(block_adapter, storage_slot_adapter)
    down_table, up_table = (
        lax.all_gather(adapter_down_weight, "store", axis=0, tiled=True),
        lax.all_gather(adapter_up_weight, "store", axis=0, tiled=True),
    )
    block_down = down_table[block_slot]
    block_up = up_table[block_slot]
    partial_sum = jnp.einsum(
        "bnd,bdk->bnk",
        feature_rows.reshape(block_count, BLOCK, shared_width),
        block_down,
        preferred_element_type=jnp.float32,
    ).reshape(block_count * BLOCK, 2 * ADAPTER_RANK)
    shrunk = lax.psum(partial_sum, ("tensor", "sub")).astype(jnp.bfloat16)
    delta = jnp.einsum(
        "bnsr,bsrc->sbnc",
        shrunk.reshape(block_count, BLOCK, 2, ADAPTER_RANK),
        block_up,
        preferred_element_type=jnp.float32,
    )
    adapter_keys = delta[0].reshape(-1, column_width)
    adapter_values = delta[1].reshape(-1, column_width)
    row_iota = jnp.arange(BLOCK, dtype=jnp.int32)
    token_positions = (block_offset[:, None] * BLOCK + row_iota[None, :]).reshape(-1)
    keys = apply_rotary(plain_keys + adapter_scale * adapter_keys, token_positions).astype(
        jnp.bfloat16
    )
    values = (plain_values + adapter_scale * adapter_values).astype(jnp.bfloat16)
    return (keys, values)


CHUNK = 32


def fused_kernel(
    n_store,
    tok_hbm, gain, kw_hbm, vw_hbm, down_hbm, up_hbm, slots, req, seg, cos_hbm, sin_hbm,
    keys_out, vals_out,
    tok, rows, kw, vw, down, up, sdown, sup, rdown, rup, acck, accv, cos_ref, sin_ref, *rest_refs,
):
    early, late = rest_refs[:6], rest_refs[6:12]
    (tok_sem, w_sem, xs_sem, xr_sem, ss_sem, sr_sem, fs_sem, fr_sem,
     ds_sem, dr_sem, us_sem, ur_sem, es_sem, er_sem) = rest_refs[12:]
    n_chunk = rows.shape[1]
    shard = n_chunk * CHUNK
    seg_count = rdown.shape[0]
    stored = down.shape[0]
    depth = down.shape[1]
    store = lax.axis_index("store")
    t = lax.axis_index("tensor")
    x, c = t // 2, t % 2
    ox, oc = 1 - x, 1 - c
    peer = {"tensor": ox * 2 + c}
    sibling = {"tensor": x * 2 + oc}
    offsets = [(n_store // 2 + j * (n_store // 2 - 1)) % n_store for j in range(seg_count)]
    remote = [j for j in range(seg_count) if offsets[j] != 0]

    def dst_of(j):
        return lax.rem(store + (n_store - offsets[j]), n_store)

    def src_of(j):
        return lax.rem(store + offsets[j], n_store)

    barrier = pltpu.get_barrier_semaphore()
    greet = [peer, sibling]
    for j in remote:
        greet += [{"store": dst_of(j)}, {"store": src_of(j)}]
    for who in greet:
        pl.semaphore_signal(barrier, inc=1, device_id=who, device_id_type=pl.DeviceIdType.MESH)

    def tok_copy(k):
        r = pl.ds(pl.multiple_of(k * CHUNK, CHUNK), CHUNK)
        return pltpu.make_async_copy(tok_hbm.at[r], tok.at[r], tok_sem.at[k])

    loads = [
        pltpu.make_async_copy(down_hbm, down, w_sem.at[0]),
        pltpu.make_async_copy(up_hbm, up, w_sem.at[1]),
        pltpu.make_async_copy(kw_hbm, kw, w_sem.at[2]),
        pltpu.make_async_copy(vw_hbm, vw, w_sem.at[3]),
        pltpu.make_async_copy(cos_hbm, cos_ref, w_sem.at[4]),
        pltpu.make_async_copy(sin_hbm, sin_ref, w_sem.at[5]),
    ]
    tok_copy(0).start()
    loads[0].start()
    loads[1].start()
    for k in range(1, n_chunk):
        tok_copy(k).start()
    for load in loads[2:]:
        load.start()

    def remote_copy(src, dst, ssem, rsem, who):
        return pltpu.make_async_remote_copy(
            src_ref=src, dst_ref=dst, send_sem=ssem, recv_sem=rsem,
            device_id=who, device_id_type=pl.DeviceIdType.MESH,
        )

    def x_copy(k):
        return remote_copy(rows.at[x, k, c], rows.at[x, k, c], xs_sem.at[k], xr_sem.at[k], peer)

    def s_copy(k):
        return remote_copy(rows.at[x, k, c], rows.at[x, k, c], ss_sem.at[k], sr_sem.at[k], sibling)

    def f_copy(k):
        return remote_copy(rows.at[ox, k, c], rows.at[ox, k, c], fs_sem.at[k], fr_sem.at[k], sibling)

    def d_copy(j):
        return remote_copy(sdown.at[j], rdown.at[j], ds_sem.at[j], dr_sem.at[j], {"store": dst_of(j)})

    def u_copy(j):
        return remote_copy(sup.at[j], rup.at[j], us_sem.at[j], ur_sem.at[j], {"store": dst_of(j)})

    def normalize(k):
        tok_copy(k).wait()

        def group(i, carry):
            r = pl.ds(pl.multiple_of(k * CHUNK + i * 16, 16), 16)
            wide = tok[r, :].astype(jnp.float32)
            factor = lax.rsqrt(jnp.mean(wide * wide, axis=1, keepdims=True) + 1e-05)
            rows[x, k, c, pl.ds(pl.multiple_of(i * 16, 16), 16), :] = (
                wide * factor * gain[...]
            ).astype(jnp.bfloat16)
            return carry

        lax.fori_loop(0, CHUNK // 16, group, 0)

    normalize(0)
    pl.semaphore_wait(barrier, len(greet))
    x_copy(0).start()
    s_copy(0).start()

    loads[0].wait()
    loads[1].wait()
    for j in range(seg_count):
        wanted = req[dst_of(j) * seg_count + j]
        local = jnp.int32(0)
        for i in range(1, stored):
            local = jnp.where(slots[store * stored + i] == wanted, jnp.int32(i), local)
        if j in remote:
            sdown[j] = down[local]
            sup[j] = up[local]
            d_copy(j).start()
        else:
            rdown[j] = down[local]
            rup[j] = up[local]

    normalize(1)
    x_copy(1).start()
    s_copy(1).start()

    def prepare(k, carry):
        normalize(k)
        s_copy(k).start()
        return carry

    lax.fori_loop(2, n_chunk, prepare, 0)

    loads[2].wait()
    loads[3].wait()

    def project(xi, k, ci, count):
        at = pl.ds(pl.multiple_of((xi * 2 + ci) * shard + k * CHUNK, CHUNK), count * CHUNK)
        lhs = rows[xi, pl.ds(k, count), ci].reshape(count * CHUNK, kw.shape[0])
        acck[at, :] = jnp.dot(lhs, kw[...], preferred_element_type=jnp.float32)
        accv[at, :] = jnp.dot(lhs, vw[...], preferred_element_type=jnp.float32)

    group = 4

    def local_rows(i, carry):
        project(x, i * group, c, group)
        return carry

    lax.fori_loop(0, n_chunk // group, local_rows, 0)

    def sibling_rows(i, carry):
        def arrived(k, inner):
            s_copy(i * group + k).wait()
            return inner

        lax.fori_loop(0, group, arrived, 0)
        project(x, i * group, oc, group)
        return carry

    lax.fori_loop(0, n_chunk // group, sibling_rows, 0)

    def project_far(k):
        lhs = rows[ox, k].reshape(2 * CHUNK, kw.shape[0])
        pk = jnp.dot(lhs, kw[...], preferred_element_type=jnp.float32)
        pv = jnp.dot(lhs, vw[...], preferred_element_type=jnp.float32)
        for ci in range(2):
            at = pl.ds(pl.multiple_of((ox * 2 + ci) * shard + k * CHUNK, CHUNK), CHUNK)
            acck[at, :] = pk[ci * CHUNK : (ci + 1) * CHUNK]
            accv[at, :] = pv[ci * CHUNK : (ci + 1) * CHUNK]

    def far_rows(k, carry):
        x_copy(k).wait()
        f_copy(k).start()

        @pl.when(k + 2 < n_chunk)
        def _():
            x_copy(k + 2).start()

        f_copy(k).wait()
        project_far(k)
        return carry

    lax.fori_loop(0, n_chunk - 2, far_rows, 0)
    for j in remote:
        u_copy(j).start()
    lax.fori_loop(n_chunk - 2, n_chunk - 1, far_rows, 0)

    def layout(b):
        end, which, first = jnp.int32(0), jnp.int32(0), jnp.int32(0)
        for j in range(seg_count):
            end = end + seg[0, j]
            past = end <= b
            which = which + jnp.where(past, jnp.int32(1), jnp.int32(0))
            first = jnp.where(past, end, first)
        return jnp.minimum(which, seg_count - 1), jnp.minimum(b - first, cos_ref.shape[0] - 1)

    per_block = BLOCK // CHUNK
    per_shard = shard // BLOCK
    feats = pl.ds(pl.multiple_of(t * depth, depth), depth)
    first_pieces = [(i, i * per_block, per_block) for i in range(per_shard)]
    first_pieces[-1] = (per_shard - 1, (per_shard - 1) * per_block, per_block - 1)
    last_pieces = [(per_shard - 1, n_chunk - 1, 1)]

    def shrink(pieces, part):
        base = pieces[0][1]

        def source(ti, carry):
            for i, k0, count in pieces:
                which, _ = layout(ti * per_shard + i)
                lhs = rows[ti // 2, k0 : k0 + count, ti % 2, :, feats].reshape(count * CHUNK, depth)
                part[ti, (k0 - base) * CHUNK : (k0 - base + count) * CHUNK, :] = jnp.dot(
                    lhs, rdown[which], preferred_element_type=jnp.float32
                )
            return carry

        lax.fori_loop(0, 4, source, 0)

    def finish(pieces, sh):
        base = pieces[0][1]

        def source(ti, carry):
            for i, k0, count in pieces:
                n = count * CHUNK
                which, place = layout(ti * per_shard + i)
                at = pl.ds(pl.multiple_of(ti * shard + k0 * CHUNK, CHUNK), n)
                start = (k0 - i * per_block) * CHUNK
                low = sh[ti, (k0 - base) * CHUNK : (k0 - base) * CHUNK + n, :]
                dk = jnp.dot(
                    low[:, :ADAPTER_RANK], rup[which, 0], preferred_element_type=jnp.float32
                )
                dv = jnp.dot(
                    low[:, ADAPTER_RANK:], rup[which, 1], preferred_element_type=jnp.float32
                )
                vals_out[at, :] = (accv[at, :] + adapter_scale * dv).astype(jnp.bfloat16)
                p = acck[at, :] + adapter_scale * dk
                cos = cos_ref[place, start : start + n, :]
                sin = sin_ref[place, start : start + n, :]
                for h in range(p.shape[1] // HD):
                    head = p[:, h * HD : (h + 1) * HD]
                    turned = head * cos + pltpu.roll(head, HD // 2, 1) * sin
                    keys_out[at, h * HD : (h + 1) * HD] = turned.astype(jnp.bfloat16)
            return carry

        lax.fori_loop(0, 4, source, 0)

    mine = pl.ds(c * 2, 2)
    others = pl.ds(oc * 2, 2)

    def pair_copy(bufs, n):
        return remote_copy(bufs[0].at[others], bufs[1], es_sem.at[n], er_sem.at[n], sibling)

    def cross_copy(bufs, n):
        return remote_copy(bufs[3], bufs[4], es_sem.at[n], er_sem.at[n], peer)

    def share_copy(bufs, n):
        return remote_copy(bufs[5].at[mine], bufs[5].at[mine], es_sem.at[n], er_sem.at[n], sibling)

    def add_pair(bufs):
        part, rs1, mid, narrow, _, _ = bufs
        mid[...] = part[mine] + rs1[...]
        narrow[...] = mid[...].astype(jnp.bfloat16)

    def add_cross(bufs):
        _, _, mid, _, rs2, sh = bufs
        sh[mine] = (mid[...] + rs2[...].astype(jnp.float32)).astype(jnp.bfloat16)

    for j in remote:
        d_copy(j).wait()
    shrink(first_pieces, early[0])
    pair_copy(early, 0).start()
    pair_copy(early, 0).wait()
    add_pair(early)
    cross_copy(early, 1).start()
    x_copy(n_chunk - 1).wait()
    f_copy(n_chunk - 1).start()
    cross_copy(early, 1).wait()
    add_cross(early)
    share_copy(early, 2).start()
    f_copy(n_chunk - 1).wait()
    shrink(last_pieces, late[0])
    pair_copy(late, 3).start()
    project_far(n_chunk - 1)
    pair_copy(late, 3).wait()
    add_pair(late)
    cross_copy(late, 4).start()
    share_copy(early, 2).wait()
    for j in remote:
        u_copy(j).wait()
    loads[4].wait()
    loads[5].wait()
    finish(first_pieces, early[5])
    cross_copy(late, 4).wait()
    add_cross(late)
    share_copy(late, 5).start()
    share_copy(late, 5).wait()
    finish(last_pieces, late[5])


def rotary_tables(blocks):
    frequency = np.float32(rope_base) ** (
        np.float32(-2.0) * np.arange(HD // 2, dtype=np.float32) / np.float32(HD)
    )
    angles = np.arange(blocks * BLOCK, dtype=np.float32)[:, None] * frequency[None, :]
    wide = angles.astype(np.float64)
    cos = np.concatenate([np.cos(wide), np.cos(wide)], axis=1).astype(np.float32)
    sin = np.concatenate([-np.sin(wide), np.sin(wide)], axis=1).astype(np.float32)
    return cos.reshape(blocks, BLOCK, HD), sin.reshape(blocks, BLOCK, HD)


def fused(
    n_store,
    tokens,
    attention_norm_gain,
    key_weight,
    value_weight,
    adapter_down_weight,
    adapter_up_weight,
    storage_slot_adapter,
    request_adapter,
    segment_blocks,
):
    shard, width = tokens.shape
    cols = key_weight.shape[1]
    total = 4 * shard
    n_chunk = shard // CHUNK
    n_block = total // BLOCK
    seg_count = segment_blocks.shape[1]
    stored, depth, ranks = adapter_down_weight.shape
    up_shape = adapter_up_weight.shape[1:]
    cos, sin = rotary_tables(n_block - seg_count + 1)
    bf16, f32 = jnp.bfloat16, jnp.float32
    any_spec = pl.BlockSpec(memory_space=pl.ANY)
    vmem = pl.BlockSpec(memory_space=pltpu.VMEM)
    smem = pl.BlockSpec(memory_space=pltpu.SMEM)
    dma = pltpu.SemaphoreType.DMA
    def exchange(n):
        return [
            pltpu.VMEM((4, n, ranks), f32),
            pltpu.VMEM((2, n, ranks), f32),
            pltpu.VMEM((2, n, ranks), f32),
            pltpu.VMEM((2, n, ranks), bf16),
            pltpu.VMEM((2, n, ranks), bf16),
            pltpu.VMEM((4, n, ranks), bf16),
        ]

    outs = [jax.ShapeDtypeStruct((total, cols), bf16)] * 2
    made = pl.pallas_call(
        functools.partial(fused_kernel, n_store),
        out_shape=outs,
        in_specs=[any_spec, vmem, any_spec, any_spec, any_spec, any_spec, smem, smem, smem, any_spec, any_spec],
        out_specs=[vmem, vmem],
        scratch_shapes=[
            pltpu.VMEM((shard, width), bf16),
            pltpu.VMEM((2, n_chunk, 2, CHUNK, width), bf16),
            pltpu.VMEM((width, cols), bf16),
            pltpu.VMEM((width, cols), bf16),
            pltpu.VMEM((stored, depth, ranks), bf16),
            pltpu.VMEM((stored,) + up_shape, bf16),
            pltpu.VMEM((seg_count, depth, ranks), bf16),
            pltpu.VMEM((seg_count,) + up_shape, bf16),
            pltpu.VMEM((seg_count, depth, ranks), bf16),
            pltpu.VMEM((seg_count,) + up_shape, bf16),
            pltpu.VMEM((total, cols), f32),
            pltpu.VMEM((total, cols), f32),
            pltpu.VMEM(cos.shape, f32),
            pltpu.VMEM(sin.shape, f32),
            *exchange(shard - CHUNK),
            *exchange(CHUNK),
            dma((n_chunk,)), dma((6,)), dma((n_chunk,)), dma((n_chunk,)), dma((n_chunk,)),
            dma((n_chunk,)), dma((n_chunk,)), dma((n_chunk,)),
            dma((seg_count,)), dma((seg_count,)), dma((seg_count,)), dma((seg_count,)),
            dma((6,)), dma((6,)),
        ],
        compiler_params=pltpu.CompilerParams(
            collective_id=0, has_side_effects=True, vmem_limit_bytes=56 * 1024 * 1024
        ),
        cost_estimate=pl.CostEstimate(
            flops=2 * total * (2 * width * cols + depth * ranks),
            bytes_accessed=2 * (shard * width + 2 * width * cols + 2 * total * cols),
            transcendentals=0,
        ),
    )(
        tokens,
        attention_norm_gain.reshape(1, width),
        key_weight,
        value_weight,
        adapter_down_weight,
        adapter_up_weight,
        storage_slot_adapter,
        request_adapter,
        segment_blocks,
        jnp.asarray(cos),
        jnp.asarray(sin),
    )
    return made


def solution(mesh):
    in_specs = (
        P(("parts", "store", "tensor"), None),
        P(),
        P(None, ("tensor", "sub")),
        P(None, ("tensor", "sub")),
        P(("parts", "store"), ("tensor", "sub"), None),
        P(("parts", "store"), None, None, ("tensor", "sub")),
        P("parts"),
        P("parts"),
        P(("parts", "store"), None),
    )
    out_specs = (P(("parts", "store"), ("tensor", "sub")), P(("parts", "store"), ("tensor", "sub")))
    body = per_device
    if mesh.shape["sub"] == 1 and mesh.shape["tensor"] == 4:
        body = functools.partial(fused, mesh.shape["store"])
    return jax.shard_map(
        body, mesh=mesh, in_specs=in_specs, out_specs=out_specs, check_vma=False
    )
```

```python
import functools

import jax
import jax.numpy as jnp
import numpy as np
from jax import lax
from jax.experimental import pallas as pl
from jax.experimental.pallas import tpu as pltpu
from jax.sharding import PartitionSpec as P

HD = 128
ADAPTER_RANK = 64
BLOCK = 128


adapter_scale = 0.5
rope_base = 500000.0


def apply_rotary(pre_rot, token_positions):
    row_count = pre_rot.shape[0]
    half_width = HD // 2
    frequency = rope_base ** (-2.0 * jnp.arange(half_width, dtype=jnp.float32) / HD)
    angles = token_positions.astype(jnp.float32)[:, None] * frequency[None, :]
    cosine_part = jnp.cos(angles)[:, None, :]
    sine_part = jnp.sin(angles)[:, None, :]
    heads = pre_rot.reshape(row_count, pre_rot.shape[1] // HD, HD)
    first_half = heads[:, :, :half_width]
    second_half = heads[:, :, half_width:]
    turned = jnp.concatenate(
        [
            first_half * cosine_part - second_half * sine_part,
            second_half * cosine_part + first_half * sine_part,
        ],
        axis=2,
    )
    return turned.reshape(row_count, pre_rot.shape[1])


def find_slots(adapter_ids, storage_slot_adapter):
    slot_iota = jnp.arange(storage_slot_adapter.shape[0], dtype=jnp.int32)
    hits = adapter_ids[..., None] == storage_slot_adapter
    return jnp.sum(jnp.where(hits, slot_iota, 0), axis=-1)


def block_layout(block_count, seg_row, group_req):
    seg_end = jnp.cumsum(seg_row)
    block_iota = jnp.arange(block_count, dtype=jnp.int32)
    which_seg = jnp.sum((seg_end[None, :] <= block_iota[:, None]).astype(jnp.int32), axis=1)
    seg_iota = jnp.arange(seg_row.shape[0], dtype=jnp.int32)
    picked = seg_iota[None, :] == which_seg[:, None]
    block_adapter = jnp.sum(jnp.where(picked, group_req[None, :], 0), axis=1)
    first_block = jnp.sum(jnp.where(picked, (seg_end - seg_row)[None, :], 0), axis=1)
    return (block_adapter, block_iota - first_block)


def per_device(
    tokens,
    attention_norm_gain,
    key_weight,
    value_weight,
    adapter_down_weight,
    adapter_up_weight,
    storage_slot_adapter,
    request_adapter,
    segment_blocks,
):
    wide = tokens.astype(jnp.float32)
    factor = lax.rsqrt(jnp.mean(wide * wide, axis=1, keepdims=True) + 1e-05)
    normed = (wide * factor * attention_norm_gain[None, :]).astype(jnp.bfloat16)
    shared_width = adapter_down_weight.shape[1]
    column_width = key_weight.shape[1]
    feature_start = lax.axis_index(("tensor", "sub")) * shared_width
    piece = lax.all_gather(normed, "tensor", axis=0, tiled=True)
    keys_part = jnp.dot(piece, key_weight, preferred_element_type=jnp.float32)
    values_part = jnp.dot(piece, value_weight, preferred_element_type=jnp.float32)
    feature_cols = lax.dynamic_slice_in_dim(piece, feature_start, shared_width, 1).astype(
        jnp.float32
    )
    gathered = jnp.concatenate([keys_part, values_part, feature_cols], axis=1)
    plain_keys = gathered[:, :column_width]
    plain_values = gathered[:, column_width : 2 * column_width]
    feature_rows = gathered[:, 2 * column_width :].astype(jnp.bfloat16)
    block_count = gathered.shape[0] // BLOCK
    seg_count = segment_blocks.shape[1]
    group = lax.axis_index("store")
    group_req = lax.dynamic_slice_in_dim(request_adapter, group * seg_count, seg_count)
    block_adapter, block_offset = block_layout(block_count, segment_blocks[0], group_req)
    block_slot = find_slots(block_adapter, storage_slot_adapter)
    down_table, up_table = (
        lax.all_gather(adapter_down_weight, "store", axis=0, tiled=True),
        lax.all_gather(adapter_up_weight, "store", axis=0, tiled=True),
    )
    block_down = down_table[block_slot]
    block_up = up_table[block_slot]
    partial_sum = jnp.einsum(
        "bnd,bdk->bnk",
        feature_rows.reshape(block_count, BLOCK, shared_width),
        block_down,
        preferred_element_type=jnp.float32,
    ).reshape(block_count * BLOCK, 2 * ADAPTER_RANK)
    shrunk = lax.psum(partial_sum, ("tensor", "sub")).astype(jnp.bfloat16)
    delta = jnp.einsum(
        "bnsr,bsrc->sbnc",
        shrunk.reshape(block_count, BLOCK, 2, ADAPTER_RANK),
        block_up,
        preferred_element_type=jnp.float32,
    )
    adapter_keys = delta[0].reshape(-1, column_width)
    adapter_values = delta[1].reshape(-1, column_width)
    row_iota = jnp.arange(BLOCK, dtype=jnp.int32)
    token_positions = (block_offset[:, None] * BLOCK + row_iota[None, :]).reshape(-1)
    keys = apply_rotary(plain_keys + adapter_scale * adapter_keys, token_positions).astype(
        jnp.bfloat16
    )
    values = (plain_values + adapter_scale * adapter_values).astype(jnp.bfloat16)
    return (keys, values)


CHUNK = 32


def fused_kernel(
    n_store,
    tok_hbm, gain, kw_hbm, vw_hbm, down_hbm, up_hbm, slots, req, seg, cos_hbm, sin_hbm,
    keys_out, vals_out,
    tok, rows, kw, vw, down, up, sdown, sup, rdown, rup, acck, accv, cos_ref, sin_ref, *rest_refs,
):
    early, late = rest_refs[:6], rest_refs[6:12]
    (tok_sem, w_sem, xs_sem, xr_sem, ss_sem, sr_sem, fs_sem, fr_sem,
     ds_sem, dr_sem, us_sem, ur_sem, es_sem, er_sem) = rest_refs[12:]
    n_chunk = rows.shape[1]
    shard = n_chunk * CHUNK
    seg_count = rdown.shape[0]
    stored = down.shape[0]
    depth = down.shape[1]
    store = lax.axis_index("store")
    t = lax.axis_index("tensor")
    x, c = t // 2, t % 2
    ox, oc = 1 - x, 1 - c
    peer = {"tensor": ox * 2 + c}
    sibling = {"tensor": x * 2 + oc}
    offsets = [(n_store // 2 + j * (n_store // 2 - 1)) % n_store for j in range(seg_count)]
    remote = [j for j in range(seg_count) if offsets[j] != 0]

    def dst_of(j):
        return lax.rem(store + (n_store - offsets[j]), n_store)

    def src_of(j):
        return lax.rem(store + offsets[j], n_store)

    barrier = pltpu.get_barrier_semaphore()
    greet = [peer, sibling]
    for j in remote:
        greet += [{"store": dst_of(j)}, {"store": src_of(j)}]
    for who in greet:
        pl.semaphore_signal(barrier, inc=1, device_id=who, device_id_type=pl.DeviceIdType.MESH)

    def tok_copy(k):
        r = pl.ds(pl.multiple_of(k * CHUNK, CHUNK), CHUNK)
        return pltpu.make_async_copy(tok_hbm.at[r], tok.at[r], tok_sem.at[k])

    loads = [
        pltpu.make_async_copy(down_hbm, down, w_sem.at[0]),
        pltpu.make_async_copy(up_hbm, up, w_sem.at[1]),
        pltpu.make_async_copy(kw_hbm, kw, w_sem.at[2]),
        pltpu.make_async_copy(vw_hbm, vw, w_sem.at[3]),
        pltpu.make_async_copy(cos_hbm, cos_ref, w_sem.at[4]),
        pltpu.make_async_copy(sin_hbm, sin_ref, w_sem.at[5]),
    ]
    tok_copy(0).start()
    loads[0].start()
    loads[1].start()
    for k in range(1, n_chunk):
        tok_copy(k).start()
    for load in loads[2:]:
        load.start()

    def remote_copy(src, dst, ssem, rsem, who):
        return pltpu.make_async_remote_copy(
            src_ref=src, dst_ref=dst, send_sem=ssem, recv_sem=rsem,
            device_id=who, device_id_type=pl.DeviceIdType.MESH,
        )

    def x_copy(k):
        return remote_copy(rows.at[x, k, c], rows.at[x, k, c], xs_sem.at[k], xr_sem.at[k], peer)

    def s_copy(k):
        return remote_copy(rows.at[x, k, c], rows.at[x, k, c], ss_sem.at[k], sr_sem.at[k], sibling)

    def f_copy(k):
        return remote_copy(rows.at[ox, k, c], rows.at[ox, k, c], fs_sem.at[k], fr_sem.at[k], sibling)

    def d_copy(j):
        return remote_copy(sdown.at[j], rdown.at[j], ds_sem.at[j], dr_sem.at[j], {"store": dst_of(j)})

    def u_copy(j):
        return remote_copy(sup.at[j], rup.at[j], us_sem.at[j], ur_sem.at[j], {"store": dst_of(j)})

    def normalize(k):
        tok_copy(k).wait()

        def group(i, carry):
            r = pl.ds(pl.multiple_of(k * CHUNK + i * 16, 16), 16)
            wide = tok[r, :].astype(jnp.float32)
            factor = lax.rsqrt(jnp.mean(wide * wide, axis=1, keepdims=True) + 1e-05)
            rows[x, k, c, pl.ds(pl.multiple_of(i * 16, 16), 16), :] = (
                wide * factor * gain[...]
            ).astype(jnp.bfloat16)
            return carry

        lax.fori_loop(0, CHUNK // 16, group, 0)

    normalize(0)
    pl.semaphore_wait(barrier, len(greet))
    x_copy(0).start()
    s_copy(0).start()

    loads[0].wait()
    loads[1].wait()
    for j in range(seg_count):
        wanted = req[dst_of(j) * seg_count + j]
        local = jnp.int32(0)
        for i in range(1, stored):
            local = jnp.where(slots[store * stored + i] == wanted, jnp.int32(i), local)
        if j in remote:
            sdown[j] = down[local]
            sup[j] = up[local]
            d_copy(j).start()
        else:
            rdown[j] = down[local]
            rup[j] = up[local]

    normalize(1)
    x_copy(1).start()
    s_copy(1).start()

    def prepare(k, carry):
        normalize(k)
        s_copy(k).start()
        return carry

    lax.fori_loop(2, n_chunk, prepare, 0)

    loads[2].wait()
    loads[3].wait()

    def project(xi, k, ci, count):
        at = pl.ds(pl.multiple_of((xi * 2 + ci) * shard + k * CHUNK, CHUNK), count * CHUNK)
        lhs = rows[xi, pl.ds(k, count), ci].reshape(count * CHUNK, kw.shape[0])
        acck[at, :] = jnp.dot(lhs, kw[...], preferred_element_type=jnp.float32)
        accv[at, :] = jnp.dot(lhs, vw[...], preferred_element_type=jnp.float32)

    group = 4

    def local_rows(i, carry):
        project(x, i * group, c, group)
        return carry

    lax.fori_loop(0, n_chunk // group, local_rows, 0)

    def sibling_rows(i, carry):
        def arrived(k, inner):
            s_copy(i * group + k).wait()
            return inner

        lax.fori_loop(0, group, arrived, 0)
        project(x, i * group, oc, group)
        return carry

    lax.fori_loop(0, n_chunk // group, sibling_rows, 0)

    def project_far(k):
        lhs = rows[ox, k].reshape(2 * CHUNK, kw.shape[0])
        pk = jnp.dot(lhs, kw[...], preferred_element_type=jnp.float32)
        pv = jnp.dot(lhs, vw[...], preferred_element_type=jnp.float32)
        for ci in range(2):
            at = pl.ds(pl.multiple_of((ox * 2 + ci) * shard + k * CHUNK, CHUNK), CHUNK)
            acck[at, :] = pk[ci * CHUNK : (ci + 1) * CHUNK]
            accv[at, :] = pv[ci * CHUNK : (ci + 1) * CHUNK]

    def far_rows(k, carry):
        x_copy(k).wait()
        f_copy(k).start()

        @pl.when(k + 2 < n_chunk)
        def _():
            x_copy(k + 2).start()

        f_copy(k).wait()
        project_far(k)
        return carry

    lax.fori_loop(0, n_chunk - 2, far_rows, 0)
    for j in remote:
        u_copy(j).start()
    x_copy(n_chunk - 2).wait()
    f_copy(n_chunk - 2).start()
    f_copy(n_chunk - 2).wait()

    def layout(b):
        end, which, first = jnp.int32(0), jnp.int32(0), jnp.int32(0)
        for j in range(seg_count):
            end = end + seg[0, j]
            past = end <= b
            which = which + jnp.where(past, jnp.int32(1), jnp.int32(0))
            first = jnp.where(past, end, first)
        return jnp.minimum(which, seg_count - 1), jnp.minimum(b - first, cos_ref.shape[0] - 1)

    per_block = BLOCK // CHUNK
    per_shard = shard // BLOCK
    feats = pl.ds(pl.multiple_of(t * depth, depth), depth)
    first_pieces = [(i, i * per_block, per_block) for i in range(per_shard)]
    first_pieces[-1] = (per_shard - 1, (per_shard - 1) * per_block, per_block - 1)
    last_pieces = [(per_shard - 1, n_chunk - 1, 1)]

    def shrink(pieces, part, first, number):
        base = pieces[0][1]

        def source(i_source, carry):
            ti = first + i_source
            for i, k0, count in pieces:
                which, _ = layout(ti * per_shard + i)
                lhs = rows[ti // 2, k0 : k0 + count, ti % 2, :, feats].reshape(count * CHUNK, depth)
                part[ti, (k0 - base) * CHUNK : (k0 - base + count) * CHUNK, :] = jnp.dot(
                    lhs, rdown[which], preferred_element_type=jnp.float32
                )
            return carry

        lax.fori_loop(0, number, source, 0)

    def finish(pieces, sh):
        base = pieces[0][1]

        def source(ti, carry):
            for i, k0, count in pieces:
                n = count * CHUNK
                which, place = layout(ti * per_shard + i)
                at = pl.ds(pl.multiple_of(ti * shard + k0 * CHUNK, CHUNK), n)
                start = (k0 - i * per_block) * CHUNK
                low = sh[ti, (k0 - base) * CHUNK : (k0 - base) * CHUNK + n, :]
                dk = jnp.dot(
                    low[:, :ADAPTER_RANK], rup[which, 0], preferred_element_type=jnp.float32
                )
                dv = jnp.dot(
                    low[:, ADAPTER_RANK:], rup[which, 1], preferred_element_type=jnp.float32
                )
                vals_out[at, :] = (accv[at, :] + adapter_scale * dv).astype(jnp.bfloat16)
                p = acck[at, :] + adapter_scale * dk
                cos = cos_ref[place, start : start + n, :]
                sin = sin_ref[place, start : start + n, :]
                for h in range(p.shape[1] // HD):
                    head = p[:, h * HD : (h + 1) * HD]
                    turned = head * cos + pltpu.roll(head, HD // 2, 1) * sin
                    keys_out[at, h * HD : (h + 1) * HD] = turned.astype(jnp.bfloat16)
            return carry

        lax.fori_loop(0, 4, source, 0)

    mine = pl.ds(c * 2, 2)
    others = pl.ds(oc * 2, 2)

    def pair_copy(bufs, n):
        return remote_copy(bufs[0].at[others], bufs[1], es_sem.at[n], er_sem.at[n], sibling)

    def cross_copy(bufs, n):
        return remote_copy(bufs[3], bufs[4], es_sem.at[n], er_sem.at[n], peer)

    def share_copy(bufs, n):
        return remote_copy(bufs[5].at[mine], bufs[5].at[mine], es_sem.at[n], er_sem.at[n], sibling)

    def add_pair(bufs):
        part, rs1, mid, narrow, _, _ = bufs
        mid[...] = part[mine] + rs1[...]
        narrow[...] = mid[...].astype(jnp.bfloat16)

    def add_cross(bufs):
        _, _, mid, _, rs2, sh = bufs
        sh[mine] = (mid[...] + rs2[...].astype(jnp.float32)).astype(jnp.bfloat16)

    for j in remote:
        d_copy(j).wait()
    shrink(first_pieces, early[0], 0, 4)
    pair_copy(early, 0).start()
    shrink(last_pieces, late[0], x * 2, 2)
    pair_copy(early, 0).wait()
    add_pair(early)
    cross_copy(early, 1).start()
    project_far(n_chunk - 2)
    x_copy(n_chunk - 1).wait()
    f_copy(n_chunk - 1).start()
    shrink(last_pieces, late[0], ox * 2 + c, 1)
    cross_copy(early, 1).wait()
    add_cross(early)
    share_copy(early, 2).start()
    f_copy(n_chunk - 1).wait()
    shrink(last_pieces, late[0], ox * 2 + oc, 1)
    pair_copy(late, 3).start()
    project_far(n_chunk - 1)
    pair_copy(late, 3).wait()
    add_pair(late)
    cross_copy(late, 4).start()
    share_copy(early, 2).wait()
    for j in remote:
        u_copy(j).wait()
    loads[4].wait()
    loads[5].wait()
    finish(first_pieces, early[5])
    cross_copy(late, 4).wait()
    add_cross(late)
    share_copy(late, 5).start()
    share_copy(late, 5).wait()
    finish(last_pieces, late[5])


def copy_kernel(a, b, c, d):
    c[...] = a[...]
    d[...] = b[...]


def rotary_tables(blocks):
    frequency = np.float32(rope_base) ** (
        np.float32(-2.0) * np.arange(HD // 2, dtype=np.float32) / np.float32(HD)
    )
    angles = np.arange(blocks * BLOCK, dtype=np.float32)[:, None] * frequency[None, :]
    wide = angles.astype(np.float64)
    cos = np.concatenate([np.cos(wide), np.cos(wide)], axis=1).astype(np.float32)
    sin = np.concatenate([-np.sin(wide), np.sin(wide)], axis=1).astype(np.float32)
    return cos.reshape(blocks, BLOCK, HD), sin.reshape(blocks, BLOCK, HD)


def fused(
    n_store,
    tokens,
    attention_norm_gain,
    key_weight,
    value_weight,
    adapter_down_weight,
    adapter_up_weight,
    storage_slot_adapter,
    request_adapter,
    segment_blocks,
):
    shard, width = tokens.shape
    cols = key_weight.shape[1]
    total = 4 * shard
    n_chunk = shard // CHUNK
    n_block = total // BLOCK
    seg_count = segment_blocks.shape[1]
    stored, depth, ranks = adapter_down_weight.shape
    up_shape = adapter_up_weight.shape[1:]
    cos, sin = rotary_tables(n_block - seg_count + 1)
    bf16, f32 = jnp.bfloat16, jnp.float32
    any_spec = pl.BlockSpec(memory_space=pl.ANY)
    vmem = pl.BlockSpec(memory_space=pltpu.VMEM)
    smem = pl.BlockSpec(memory_space=pltpu.SMEM)
    dma = pltpu.SemaphoreType.DMA
    def exchange(n):
        return [
            pltpu.VMEM((4, n, ranks), f32),
            pltpu.VMEM((2, n, ranks), f32),
            pltpu.VMEM((2, n, ranks), f32),
            pltpu.VMEM((2, n, ranks), bf16),
            pltpu.VMEM((2, n, ranks), bf16),
            pltpu.VMEM((4, n, ranks), bf16),
        ]

    outs = [jax.ShapeDtypeStruct((total, cols), bf16)] * 2
    made = pl.pallas_call(
        functools.partial(fused_kernel, n_store),
        out_shape=outs,
        in_specs=[any_spec, vmem, any_spec, any_spec, any_spec, any_spec, smem, smem, smem, any_spec, any_spec],
        out_specs=[vmem, vmem],
        scratch_shapes=[
            pltpu.VMEM((shard, width), bf16),
            pltpu.VMEM((2, n_chunk, 2, CHUNK, width), bf16),
            pltpu.VMEM((width, cols), bf16),
            pltpu.VMEM((width, cols), bf16),
            pltpu.VMEM((stored, depth, ranks), bf16),
            pltpu.VMEM((stored,) + up_shape, bf16),
            pltpu.VMEM((seg_count, depth, ranks), bf16),
            pltpu.VMEM((seg_count,) + up_shape, bf16),
            pltpu.VMEM((seg_count, depth, ranks), bf16),
            pltpu.VMEM((seg_count,) + up_shape, bf16),
            pltpu.VMEM((total, cols), f32),
            pltpu.VMEM((total, cols), f32),
            pltpu.VMEM(cos.shape, f32),
            pltpu.VMEM(sin.shape, f32),
            *exchange(shard - CHUNK),
            *exchange(CHUNK),
            dma((n_chunk,)), dma((6,)), dma((n_chunk,)), dma((n_chunk,)), dma((n_chunk,)),
            dma((n_chunk,)), dma((n_chunk,)), dma((n_chunk,)),
            dma((seg_count,)), dma((seg_count,)), dma((seg_count,)), dma((seg_count,)),
            dma((6,)), dma((6,)),
        ],
        compiler_params=pltpu.CompilerParams(
            collective_id=0, has_side_effects=True, vmem_limit_bytes=56 * 1024 * 1024
        ),
        cost_estimate=pl.CostEstimate(
            flops=2 * total * (2 * width * cols + depth * ranks),
            bytes_accessed=2 * (shard * width + 2 * width * cols + 2 * total * cols),
            transcendentals=0,
        ),
    )(
        tokens,
        attention_norm_gain.reshape(1, width),
        key_weight,
        value_weight,
        adapter_down_weight,
        adapter_up_weight,
        storage_slot_adapter,
        request_adapter,
        segment_blocks,
        jnp.asarray(cos),
        jnp.asarray(sin),
    )
    block = pl.BlockSpec((total // 2, cols), lambda i: (i, 0))
    return pl.pallas_call(
        copy_kernel,
        grid=(2,),
        out_shape=outs,
        in_specs=[block, block],
        out_specs=[block, block],
    )(*made)


def solution(mesh):
    in_specs = (
        P(("parts", "store", "tensor"), None),
        P(),
        P(None, ("tensor", "sub")),
        P(None, ("tensor", "sub")),
        P(("parts", "store"), ("tensor", "sub"), None),
        P(("parts", "store"), None, None, ("tensor", "sub")),
        P("parts"),
        P("parts"),
        P(("parts", "store"), None),
    )
    out_specs = (P(("parts", "store"), ("tensor", "sub")), P(("parts", "store"), ("tensor", "sub")))
    body = per_device
    if mesh.shape["sub"] == 1 and mesh.shape["tensor"] == 4:
        body = functools.partial(fused, mesh.shape["store"])
    return jax.shard_map(
        body, mesh=mesh, in_specs=in_specs, out_specs=out_specs, check_vma=False
    )
```
